512 devices in a mesh: fsdp: 16 (over x_hi, z), ctx: 32 (over x_lo, y, core).
Axes of the slice: x: 4 (x_hi: 2, x_lo: 2; x = x_hi * 2 + x_lo), y: 8, z: 8, core: 2. Of those that a mesh axis runs over, the one named last changes fastest.
Arguments:
- gate_value: bfloat16 [65536, 4096], P('ctx', 'fsdp'), may hold values from -6 to 6
- conv_input: bfloat16 [65536, 4096], P('ctx', 'fsdp'), may hold values from -6 to 6
- output_grad: bfloat16 [65536, 4096], P('ctx', 'fsdp'), may hold values from -6 to 6
- decay_rate: float32 [4096, 16], P(('fsdp', 'ctx')), may hold values from 1.5258789e-06 to 0.04
- residue: float32 [4096, 16], P(('fsdp', 'ctx')), may hold values from -0.3 to 0.3
Outputs:
- input_grad: bfloat16 [65536, 4096], P('ctx', 'fsdp')
- residue_grad: float32 [4096, 16], P(('fsdp', 'ctx'))
The draws below stay inside these ranges and needn't reach their ends.
All inputs are finite; a program needn't handle non-finite values.
Results may differ from the reference program's by a relative error of at most 0.0049.
Values may be sent and summed in bfloat16 or wider, within the bound.
A program may use at most 64 MiB of HBM per device.

```python
import math
import jax
import jax.numpy as jnp
from jax import lax

C = 4096
R = 16
L = 65536


def rates_of(key, fast_share, slow_floor):
    shape = (C, R)
    pick_key, fast_key, slow_key = jax.random.split(key, 3)
    picker = jax.random.uniform(pick_key, shape, jnp.float32)
    fast_rate = jnp.exp(jax.random.uniform(fast_key, shape, jnp.float32, math.log(1.0 / 50.0), math.log(1.0 / 25.0)))
    slow_rate = jnp.exp(jax.random.uniform(slow_key, shape, jnp.float32, math.log(slow_floor / L), math.log(2.0 / L)))
    return jnp.where(picker < fast_share, fast_rate, slow_rate)


def draw_decay_rate(key, part):
    rates = rates_of(key, 0.5, 0.25)
    return rates


def draw_residue(key, part):
    rates = rates_of(key, 0.5, 0.25)
    key = jax.random.fold_in(key, 7)
    noise = jax.random.truncated_normal(key, -4.0, 4.0, (C, R), jnp.float32)
    return noise * 0.25 * jnp.sqrt(2.0 * rates)


def raised(result, key, source, target, shards_of, factor):
    owner, partner = [(jnp.arange(result.shape[axis_at]) // (result.shape[axis_at] // shards_of)).reshape([-1 if axis == axis_at else 1 for axis in range(result.ndim)]) for axis_at in (source, target)]
    chosen = jax.random.permutation(key, shards_of)[partner]
    strong = (owner == chosen) | (owner == (partner + shards_of // 2) % shards_of)
    return jnp.where(strong, factor * result, result)


def block_levels(own_key, shape, cuts, low, top_value):
    level, own = 1.0, jax.random.fold_in(own_key, 6)
    for position, shards_of in cuts:
        steps = jnp.exp(jax.random.uniform(jax.random.fold_in(own, position), (shards_of,), jnp.float32, low / len(cuts), top_value / len(cuts)))
        level = level * jnp.repeat(steps, shape[position] // shards_of).reshape([-1 if axis == position else 1 for axis in range(len(shape))])
    return level


def gaussian(key, extent, scale, most, pieces=(), held_as=jnp.bfloat16):
    entries = scale * jax.random.normal(key, extent, jnp.float32)
    if pieces:
        entries = entries * block_levels(key, extent, pieces, -0.22, 0.18)
    return jnp.clip(entries, -most, most).astype(held_as)


def heavy_noise(rng, shape, scale, most, shards, heavy, kind=jnp.bfloat16):
    drawn = scale * jax.random.normal(rng, shape, jnp.float32)
    if shards:
        drawn = drawn * block_levels(rng, shape, shards, -0.22, 0.18)
    return jnp.clip(raised(drawn, jax.random.fold_in(rng, 3), *heavy), -most, most).astype(kind)


def setup_inputs(seed: int = 0) -> dict:
    key_of = jax.random.split(jax.random.key(seed), 6)
    return {
        "gate_value": gaussian(key_of[0], (L, C), 1.0, 6.0, ((0, 32), (1, 16))),
        "conv_input": gaussian(key_of[1], (L, C), 1.0, 6.0, ((0, 32), (1, 16))),
        "output_grad": heavy_noise(key_of[2], (L, C), 1.0, 6.0, ((0, 32), (1, 16)), (0, 1, 32, 2.75)),
        "decay_rate": draw_decay_rate(jax.random.fold_in(key_of[5], 71), 0),
        "residue": draw_residue(jax.random.fold_in(key_of[5], 71), 0),
    }


def reference(gate_value, conv_input, output_grad, decay_rate, residue):
    block = min(128, C)
    count = C // block
    lag_index = jnp.arange(L, dtype=jnp.float32)[:, None]

    def one_block(operands):
        gate_part, input_part, grad_part, rates, weights = operands
        taps = jnp.zeros((L, block), jnp.float32)
        for column in range(R):
            taps = taps + weights[:, column][None] * jnp.exp(-rates[:, column][None] * lag_index)
        taps_freq = jnp.fft.rfft(taps, n=2 * L, axis=0)
        rounded = lax.optimization_barrier((grad_part.astype(jnp.float32) * gate_part.astype(jnp.float32)).astype(jnp.bfloat16))
        scaled = rounded.astype(jnp.float32)
        scaled_freq = jnp.fft.rfft(scaled, n=2 * L, axis=0)
        input_freq = jnp.fft.rfft(input_part.astype(jnp.float32), n=2 * L, axis=0)
        grads = jnp.fft.irfft(scaled_freq * jnp.conj(taps_freq), n=2 * L, axis=0)[:L]
        lagged = jnp.fft.irfft(scaled_freq * jnp.conj(input_freq), n=2 * L, axis=0)[:L]
        sums = [jnp.sum(lagged * jnp.exp(-rates[:, column][None] * lag_index), axis=0) for column in range(R)]
        return grads.astype(jnp.bfloat16), jnp.stack(sums, axis=1)

    def split(array):
        return array.reshape(L, count, block).transpose(1, 0, 2)

    grads, sums = lax.map(one_block, (split(gate_value), split(conv_input), split(output_grad), decay_rate.reshape(count, block, R), residue.reshape(count, block, R)))
    return grads.transpose(1, 0, 2).reshape(L, C), sums.reshape(C, R) / L
```

```python
import functools
import math

import jax
import jax.numpy as jnp
import numpy as np
from jax import lax
from jax.experimental import pallas as pl
from jax.experimental.pallas import tpu as pltpu
from jax.sharding import PartitionSpec as P

WIDTH = 32
TERMS = 8
CHUNKS = 8
CENTER = (WIDTH - 1) / 2
MESH = pl.DeviceIdType.MESH
f32 = jnp.float32
bf16 = jnp.bfloat16


def chebyshev(z):
    rows = [np.ones_like(z), z]
    while len(rows) < TERMS:
        rows.append(2 * z * rows[-1] - rows[-2])
    return np.stack(rows)


def tables():
    i = np.arange(WIDTH)
    basis = chebyshev((i - CENTER) / (WIDTH / 2))
    lag = i[None, :] - i[:, None]
    tri = np.where(lag >= 0, basis[:, np.maximum(lag, 0)], 0.0)
    size = CHUNKS * WIDTH
    inner = np.zeros((TERMS, size, size))
    moment = np.zeros((TERMS, CHUNKS, size))
    for j in range(CHUNKS):
        part = slice(j * WIDTH, (j + 1) * WIDTH)
        inner[:, part, part] = tri
        moment[:, j, part] = basis
    moment = moment.reshape(TERMS * CHUNKS, size)
    spread = np.concatenate([moment.T, moment.T], axis=1)
    return [np.asarray(a, np.float32).astype(jnp.bfloat16) for a in (inner, moment, spread)]


def shift_rows(v, by):
    rows = v.shape[0]
    return jnp.concatenate([v[by:], jnp.zeros((by, v.shape[1]), v.dtype)], axis=0)


def kernel(
    n, length,
    gate, xin, ograd, rate, resid, inner, moment, spread,
    out, rgrad,
    g_v, x_v, o_v, s_v, out_v, inner_v, moment_v, spread_v,
    pack, rates, m_s, n_s, gacc, tau, en, fx, fo, lam_s, a32_s, a256_s, lamh_s,
    sq, cin, p256, st, yin,
    sbuf, ntbuf, ubuf, rbuf, sgot, ntgot, ugot, rgot, rgt,
    in_sem, tab_sem, out_sem,
    rates_send, rates_recv, s_send, s_recv, nt_send, nt_recv, u_send, u_recv, r_send, r_recv,
):
    me = lax.axis_index("ctx")
    half, mode = me // 16, me % 16
    steps = g_v.shape[0]

    def others(body):
        def step(i, carry):
            body(lax.rem(me + i, n))
            return carry
        lax.fori_loop(1, n, step, 0)

    barrier = pltpu.get_barrier_semaphore()
    others(lambda e: pl.semaphore_signal(barrier, inc=1, device_id={"ctx": e}, device_id_type=MESH))

    tabs = [
        pltpu.make_async_copy(moment, moment_v, tab_sem.at[0]),
        pltpu.make_async_copy(inner, inner_v, tab_sem.at[1]),
        pltpu.make_async_copy(spread, spread_v, tab_sem.at[2]),
    ]

    def fetch(q):
        return [
            pltpu.make_async_copy(src.at[:, q], dst.at[q], in_sem.at[k, q])
            for k, (src, dst) in enumerate(((gate, g_v), (ograd, o_v), (xin, x_v)))
        ]

    tabs[0].start()
    for c in fetch(0):
        c.start()
    tabs[1].start()
    for q in range(1, steps):
        for c in fetch(q):
            c.start()
    tabs[2].start()

    pack[:, 0:16] = rate[...]
    pack[:, 16:32] = resid[...]
    mine = pl.ds(pl.multiple_of(me * 8, 8), 8)
    rates[mine] = pack[...]
    pl.semaphore_wait(barrier, n - 1)

    def send_rates(e):
        pltpu.make_async_remote_copy(
            pack, rates.at[mine], rates_send, rates_recv, device_id={"ctx": e}, device_id_type=MESH
        ).start()

    others(send_rates)

    for k in range(TERMS):
        gacc[k] = jnp.zeros_like(gacc[k])
    tabs[0].wait()
    tabs[1].wait()

    def first(q, carry):
        for c in fetch(q):
            c.wait()
        s = (o_v[q].astype(f32) * g_v[q].astype(f32)).astype(bf16).reshape(256, 256)
        x = x_v[q].reshape(256, 256)
        s_v[q] = s
        m_s[q] = jnp.dot(moment_v[...], s, preferred_element_type=f32)
        n_s[q] = jnp.dot(moment_v[...], x, preferred_element_type=f32)
        wide = x.astype(f32)
        for k in range(TERMS):
            near = jnp.dot(inner_v[k], s, preferred_element_type=f32)
            gacc[k] += jnp.sum((near * wide).reshape(32, 8, 256), axis=0)
        return carry

    lax.fori_loop(0, steps, first, 0)

    pltpu.make_async_copy(rates.at[pl.ds(0, 8 * (n - 1))], rates.at[pl.ds(0, 8 * (n - 1))], rates_recv).wait()
    turned = rates[...].T
    lam, res = turned[0:16], turned[16:32]
    lam_s[...] = lam
    lamh_s[0:16] = lam[:, 0:128]
    lamh_s[16:32] = lam[:, 128:256]
    a32_s[...] = jnp.exp(-WIDTH * lam)
    a256_s[...] = jnp.exp(-(WIDTH * steps) * lam)
    ahead = jnp.exp(-CENTER * lam)
    behind = jnp.exp(-(WIDTH - CENTER) * lam)
    h = lam * (WIDTH / 4)
    w = h * h
    power = jnp.ones_like(h)
    for k in range(TERMS):
        tail = 1.0 + w * (1.0 / (4 * (k + 4)))
        for m in (3, 2, 1):
            tail = 1.0 + w * tail * (1.0 / (m * (k + m)))
        term = power * tail * ((1.0 if k == 0 else 2.0) / math.factorial(k))
        e = ahead * (term if k % 2 == 0 else -term)
        b = behind * term
        en[k] = e
        fx[k] = b
        fo[k] = b * res
        tau[k] = jnp.sum(e * res, axis=0, keepdims=True)
        power = power * h

    def scan(r, carry):
        row = pl.ds(r, 1)
        e = [en[k, row, :] for k in range(TERMS)]
        a = a32_s[row, :]
        u = None
        for q in reversed(range(steps)):
            new = e[0] * m_s[q, 0:8]
            for k in range(1, TERMS):
                new = new + e[k] * m_s[q, 8 * k : 8 * k + 8]
            sq[q, r] = new
            u = new if u is None else new + a * u
        big = a256_s[row, :]
        for by in (1, 2, 4):
            u = u + big * shift_rows(u, by)
            big = big * big
        sbuf[r] = u[0:1, 0:128]
        sbuf[16 + r] = u[0:1, 128:256]
        cin[r] = shift_rows(u, 1)
        return carry

    lax.fori_loop(0, 16, scan, 0)
    sgot[me] = sbuf[me]

    def send_rows(src, dst, send, recv):
        def body(e):
            pltpu.make_async_remote_copy(
                src.at[e], dst.at[me], send, recv, device_id={"ctx": e}, device_id_type=MESH
            ).start()
        return body

    def arrived(ref, sem):
        view = ref.at[pl.ds(0, n - 1)]
        pltpu.make_async_copy(view, view, sem).wait()

    others(send_rows(sbuf, sgot, s_send, s_recv))

    behind_chunks = (7 - lax.broadcasted_iota(jnp.int32, (8, 256), 0)).astype(f32) * (-float(WIDTH * steps))
    gsum = [jnp.sum(gacc[k], axis=0, keepdims=True) for k in range(TERMS)]

    def share(r, carry):
        row = pl.ds(r, 1)
        f = [fx[k, row, :] for k in range(TERMS)]
        a = a32_s[row, :]
        reach = jnp.exp(behind_chunks * lam_s[row, :])
        p256[r] = reach
        u = cin[r]
        acc = jnp.zeros((8, 256), f32)
        tail = jnp.zeros((8, 256), f32)
        fall = jnp.ones((1, 256), f32)
        for q in reversed(range(steps)):
            v = f[0] * n_s[q, 0:8]
            for k in range(1, TERMS):
                v = v + f[k] * n_s[q, 8 * k : 8 * k + 8]
            acc = acc + v * u
            tail = tail + v * fall
            if q:
                u = sq[q, r] + a * u
                fall = fall * a
        near = jnp.sum(acc, axis=0, keepdims=True)
        for k in range(TERMS):
            near = near + en[k, row, :] * gsum[k]
        tail = jnp.sum(tail * reach, axis=0, keepdims=True)
        ntbuf[r, 0:1] = near[:, 0:128]
        ntbuf[16 + r, 0:1] = near[:, 128:256]
        ntbuf[r, 1:2] = tail[:, 0:128]
        ntbuf[16 + r, 1:2] = tail[:, 128:256]
        return carry

    lax.fori_loop(0, 16, share, 0)
    ntgot[me] = ntbuf[me]
    others(send_rows(ntbuf, ntgot, nt_send, nt_recv))

    arrived(sgot, s_recv)
    v = sgot[:, 0, :]
    big = jnp.exp(lamh_s[pl.ds(me, 1), :] * (-float(WIDTH * steps * CHUNKS)))
    for by in (1, 2, 4, 8, 16):
        v = v + big * shift_rows(v, by)
        big = big * big
    v = shift_rows(v, 1)
    ubuf[:, 0, :] = v
    ugot[me] = ubuf[me]
    others(send_rows(ubuf, ugot, u_send, u_recv))

    arrived(ntgot, nt_recv)
    total = jnp.sum(ntgot[:, 0, :] + ntgot[:, 1, :] * v, axis=0, keepdims=True) * (1.0 / length)
    rbuf[...] = total
    rgot[mode] = total

    def send_total(i, carry):
        e = half * 16 + lax.rem(mode + i, 16)
        pltpu.make_async_remote_copy(
            rbuf, rgot.at[mode], r_send, r_recv, device_id={"ctx": e}, device_id_type=MESH
        ).start()
        return carry

    lax.fori_loop(1, 16, send_total, 0)

    def within(q, carry):
        s = s_v[q]
        acc = tau[0] * jnp.dot(inner_v[0], s, preferred_element_type=f32)
        for k in range(1, TERMS):
            acc = acc + tau[k] * jnp.dot(inner_v[k], s, preferred_element_type=f32)
        yin[q] = acc
        return carry

    lax.fori_loop(0, steps, within, 0)
    tabs[2].wait()

    arrived(ugot, u_recv)
    for r in range(16):
        u = jnp.concatenate([ugot[r], ugot[16 + r]], axis=1)
        st[r] = cin[r] + p256[r] * u

    def emit(q):
        return pltpu.make_async_copy(out_v.at[q], out.at[:, q], out_sem.at[q])

    def last(i, carry):
        q = steps - 1 - i
        levels = [jnp.zeros((8, 256), f32)] * TERMS
        for r in range(16):
            u = st[r]
            for k in range(TERMS):
                levels[k] = levels[k] + fo[k, r : r + 1, :] * u
            st[r] = sq[q, r] + a32_s[r : r + 1, :] * u
        level = jnp.concatenate(levels, axis=0)
        high = level.astype(bf16)
        low = (level - high.astype(f32)).astype(bf16)
        both = jnp.concatenate([high, low], axis=0)
        y = yin[q] + jnp.dot(spread_v[...], both, preferred_element_type=f32)
        out_v[q] = y.astype(bf16).reshape(CHUNKS, WIDTH, 256)
        emit(q).start()
        return carry

    lax.fori_loop(0, steps, last, 0)

    view = rgot.at[pl.ds(0, 15)]
    pltpu.make_async_copy(view, view, r_recv).wait()
    rgt[:, 0:16] = rgot[:, 0, :].T
    rgrad[...] = rgt[pl.ds(pl.multiple_of(mode * 8, 8), 8), 0:16]

    view = rates.at[pl.ds(0, 8 * (n - 1))]
    pltpu.make_async_copy(view, view, rates_send).wait()
    arrived(sbuf, s_send)
    arrived(ntbuf, nt_send)
    arrived(ubuf, u_send)
    view = rgot.at[pl.ds(0, 15)]
    pltpu.make_async_copy(view, view, r_send).wait()
    for q in range(steps):
        emit(q).wait()


def local(inner, moment, spread, gate_value, conv_input, output_grad, decay_rate, residue):
    tokens, channels = gate_value.shape
    n = lax.axis_size("ctx")
    steps = tokens // (CHUNKS * WIDTH)
    cut = (CHUNKS, steps, WIDTH, channels)
    V = pltpu.VMEM
    dma = pltpu.SemaphoreType.DMA
    blocks = (steps, CHUNKS, WIDTH, channels)
    size = CHUNKS * WIDTH
    scratch = [
        V(blocks, bf16), V(blocks, bf16), V(blocks, bf16), V((steps, size, channels), bf16), V(blocks, bf16),
        V(inner.shape, bf16), V(moment.shape, bf16), V(spread.shape, bf16),
        V((8, 128), f32), V((8 * n, 128), f32),
        V((steps, TERMS * CHUNKS, channels), f32), V((steps, TERMS * CHUNKS, channels), f32),
        V((TERMS, 8, channels), f32), V((TERMS, 1, channels), f32),
        V((TERMS, 16, channels), f32), V((TERMS, 16, channels), f32), V((TERMS, 16, channels), f32),
        V((16, channels), f32), V((16, channels), f32), V((16, channels), f32), V((32, 128), f32),
        V((steps, 16, 8, channels), f32), V((16, 8, channels), f32), V((16, 8, channels), f32), V((16, 8, channels), f32),
        V((steps, size, channels), f32),
        V((n, 1, 128), f32), V((n, 2, 128), f32), V((n, 1, 128), f32), V((1, 128), f32),
        V((n, 1, 128), f32), V((n, 2, 128), f32), V((n, 1, 128), f32), V((16, 1, 128), f32), V((128, 128), f32),
        dma((3, steps)), dma((3,)), dma((steps,)),
    ] + [dma] * 10
    vmem_spec = pl.BlockSpec(memory_space=pltpu.VMEM)
    any_spec = pl.BlockSpec(memory_space=pl.ANY)
    out, rgrad = pl.pallas_call(
        functools.partial(kernel, n, tokens * n),
        out_shape=(jax.ShapeDtypeStruct(cut, bf16), jax.ShapeDtypeStruct(residue.shape, f32)),
        in_specs=[any_spec] * 3 + [vmem_spec] * 2 + [any_spec] * 3,
        out_specs=(any_spec, vmem_spec),
        scratch_shapes=scratch,
        compiler_params=pltpu.CompilerParams(
            collective_id=0, has_side_effects=True, vmem_limit_bytes=48 * 1024 * 1024
        ),
    )(
        gate_value.reshape(cut), conv_input.reshape(cut), output_grad.reshape(cut),
        decay_rate, residue, inner, moment, spread,
    )
    return out.reshape(tokens, channels), rgrad


def solution(mesh):
    consts = tables()
    in_specs = (P(), P(), P()) + (P("ctx", "fsdp"),) * 3 + (P(("fsdp", "ctx"), None),) * 2
    out_specs = (P("ctx", "fsdp"), P(("fsdp", "ctx"), None))
    mapped = jax.shard_map(local, mesh=mesh, in_specs=in_specs, out_specs=out_specs, check_vma=False)

    def run(*args):
        return mapped(*[jnp.asarray(c) for c in consts], *args)

    return run
```

```python
import functools
import math

import jax
import jax.numpy as jnp
import numpy as np
from jax import lax
from jax.experimental import pallas as pl
from jax.experimental.pallas import tpu as pltpu
from jax.sharding import PartitionSpec as P

WIDTH = 32
TERMS = 8
CHUNKS = 8
CENTER = (WIDTH - 1) / 2
MESH = pl.DeviceIdType.MESH
f32 = jnp.float32
bf16 = jnp.bfloat16


def chebyshev(z):
    rows = [np.ones_like(z), z]
    while len(rows) < TERMS:
        rows.append(2 * z * rows[-1] - rows[-2])
    return np.stack(rows)


def tables():
    i = np.arange(WIDTH)
    basis = chebyshev((i - CENTER) / (WIDTH / 2))
    lag = i[None, :] - i[:, None]
    tri = np.where(lag >= 0, basis[:, np.maximum(lag, 0)], 0.0)
    size = CHUNKS * WIDTH
    inner = np.zeros((TERMS, size, size))
    moment = np.zeros((TERMS, CHUNKS, size))
    for j in range(CHUNKS):
        part = slice(j * WIDTH, (j + 1) * WIDTH)
        inner[:, part, part] = tri
        moment[:, j, part] = basis
    moment = moment.reshape(TERMS * CHUNKS, size)
    spread = np.concatenate([moment.T, moment.T], axis=1)
    return [np.asarray(a, np.float32).astype(jnp.bfloat16) for a in (inner, moment, spread)]


def shift_rows(v, by):
    rows = v.shape[0]
    return jnp.concatenate([v[by:], jnp.zeros((by, v.shape[1]), v.dtype)], axis=0)


def kernel(
    n, length,
    gate, xin, ograd, rate, resid, inner, moment, spread,
    out, rgrad,
    g_v, x_v, o_v, s_v, inner_v, moment_v, spread_v, rate_v, resid_v,
    pack, rates, m_s, n_s, gacc, tau, en, fx, fo, lam_s, a32_s, a256_s, lamh_s,
    sq, cin, p256, st, yin,
    sbuf, ntbuf, ubuf, rbuf, sgot, ntgot, ugot, rgot, rgt,
    in_sem, tab_sem, par_sem,
    rates_send, rates_recv, s_send, s_recv, nt_send, nt_recv, u_send, u_recv, r_send, r_recv,
):
    me = lax.axis_index("ctx")
    half, mode = me // 16, me % 16
    steps = g_v.shape[0]

    def others(body):
        def step(i, carry):
            body(lax.rem(me + i, n))
            return carry
        lax.fori_loop(1, n, step, 0)

    barrier = pltpu.get_barrier_semaphore()
    others(lambda e: pl.semaphore_signal(barrier, inc=1, device_id={"ctx": e}, device_id_type=MESH))

    par = [pltpu.make_async_copy(rate, rate_v, par_sem.at[0]), pltpu.make_async_copy(resid, resid_v, par_sem.at[1])]
    for c in par:
        c.start()
    tabs = [
        pltpu.make_async_copy(moment, moment_v, tab_sem.at[0]),
        pltpu.make_async_copy(inner, inner_v, tab_sem.at[1]),
        pltpu.make_async_copy(spread, spread_v, tab_sem.at[2]),
    ]

    def fetch(q):
        return [
            pltpu.make_async_copy(src.at[:, q], dst.at[q], in_sem.at[k, q])
            for k, (src, dst) in enumerate(((gate, g_v), (ograd, o_v), (xin, x_v)))
        ]

    tabs[0].start()
    for c in fetch(0):
        c.start()
    tabs[1].start()
    for q in range(1, steps):
        for c in fetch(q):
            c.start()
    tabs[2].start()

    for c in par:
        c.wait()
    pack[:, 0:16] = rate_v[...]
    pack[:, 16:32] = resid_v[...]
    mine = pl.ds(pl.multiple_of(me * 8, 8), 8)
    rates[mine] = pack[...]
    pl.semaphore_wait(barrier, n - 1)

    def send_rates(e):
        pltpu.make_async_remote_copy(
            pack, rates.at[mine], rates_send, rates_recv, device_id={"ctx": e}, device_id_type=MESH
        ).start()

    others(send_rates)

    for k in range(TERMS):
        gacc[k] = jnp.zeros_like(gacc[k])
    tabs[0].wait()
    tabs[1].wait()

    def first(q, carry):
        for c in fetch(q):
            c.wait()
        s = (o_v[q].astype(f32) * g_v[q].astype(f32)).astype(bf16).reshape(256, 256)
        x = x_v[q].reshape(256, 256)
        s_v[q] = s
        m_s[q] = jnp.dot(moment_v[...], s, preferred_element_type=f32)
        n_s[q] = jnp.dot(moment_v[...], x, preferred_element_type=f32)
        wide = x.astype(f32)
        for k in range(TERMS):
            near = jnp.dot(inner_v[k], s, preferred_element_type=f32)
            gacc[k] += jnp.sum((near * wide).reshape(32, 8, 256), axis=0)
        return carry

    lax.fori_loop(0, steps, first, 0)

    pltpu.make_async_copy(rates.at[pl.ds(0, 8 * (n - 1))], rates.at[pl.ds(0, 8 * (n - 1))], rates_recv).wait()
    turned = rates[...].T
    lam, res = turned[0:16], turned[16:32]
    lam_s[...] = lam
    lamh_s[0:16] = lam[:, 0:128]
    lamh_s[16:32] = lam[:, 128:256]
    a32_s[...] = jnp.exp(-WIDTH * lam)
    a256_s[...] = jnp.exp(-(WIDTH * steps) * lam)
    ahead = jnp.exp(-CENTER * lam)
    behind = jnp.exp(-(WIDTH - CENTER) * lam)
    h = lam * (WIDTH / 4)
    w = h * h
    power = jnp.ones_like(h)
    for k in range(TERMS):
        tail = 1.0 + w * (1.0 / (4 * (k + 4)))
        for m in (3, 2, 1):
            tail = 1.0 + w * tail * (1.0 / (m * (k + m)))
        term = power * tail * ((1.0 if k == 0 else 2.0) / math.factorial(k))
        e = ahead * (term if k % 2 == 0 else -term)
        b = behind * term
        en[k] = e
        fx[k] = b
        fo[k] = b * res
        tau[k] = jnp.sum(e * res, axis=0, keepdims=True)
        power = power * h

    def scan(r, carry):
        row = pl.ds(r, 1)
        e = [en[k, row, :] for k in range(TERMS)]
        a = a32_s[row, :]
        u = None
        for q in reversed(range(steps)):
            new = e[0] * m_s[q, 0:8]
            for k in range(1, TERMS):
                new = new + e[k] * m_s[q, 8 * k : 8 * k + 8]
            sq[q, r] = new
            u = new if u is None else new + a * u
        big = a256_s[row, :]
        for by in (1, 2, 4):
            u = u + big * shift_rows(u, by)
            big = big * big
        sbuf[r] = u[0:1, 0:128]
        sbuf[16 + r] = u[0:1, 128:256]
        cin[r] = shift_rows(u, 1)
        return carry

    lax.fori_loop(0, 16, scan, 0)
    sgot[me] = sbuf[me]

    def send_rows(src, dst, send, recv):
        def body(e):
            pltpu.make_async_remote_copy(
                src.at[e], dst.at[me], send, recv, device_id={"ctx": e}, device_id_type=MESH
            ).start()
        return body

    def arrived(ref, sem):
        view = ref.at[pl.ds(0, n - 1)]
        pltpu.make_async_copy(view, view, sem).wait()

    others(send_rows(sbuf, sgot, s_send, s_recv))

    behind_chunks = (7 - lax.broadcasted_iota(jnp.int32, (8, 256), 0)).astype(f32) * (-float(WIDTH * steps))
    gsum = [jnp.sum(gacc[k], axis=0, keepdims=True) for k in range(TERMS)]

    def share(r, carry):
        row = pl.ds(r, 1)
        f = [fx[k, row, :] for k in range(TERMS)]
        a = a32_s[row, :]
        reach = jnp.exp(behind_chunks * lam_s[row, :])
        p256[r] = reach
        u = cin[r]
        acc = jnp.zeros((8, 256), f32)
        tail = jnp.zeros((8, 256), f32)
        fall = jnp.ones((1, 256), f32)
        for q in reversed(range(steps)):
            v = f[0] * n_s[q, 0:8]
            for k in range(1, TERMS):
                v = v + f[k] * n_s[q, 8 * k : 8 * k + 8]
            acc = acc + v * u
            tail = tail + v * fall
            if q:
                u = sq[q, r] + a * u
                fall = fall * a
        near = jnp.sum(acc, axis=0, keepdims=True)
        for k in range(TERMS):
            near = near + en[k, row, :] * gsum[k]
        tail = jnp.sum(tail * reach, axis=0, keepdims=True)
        ntbuf[r, 0:1] = near[:, 0:128]
        ntbuf[16 + r, 0:1] = near[:, 128:256]
        ntbuf[r, 1:2] = tail[:, 0:128]
        ntbuf[16 + r, 1:2] = tail[:, 128:256]
        return carry

    lax.fori_loop(0, 16, share, 0)
    ntgot[me] = ntbuf[me]
    others(send_rows(ntbuf, ntgot, nt_send, nt_recv))

    arrived(sgot, s_recv)
    v = sgot[:, 0, :]
    big = jnp.exp(lamh_s[pl.ds(me, 1), :] * (-float(WIDTH * steps * CHUNKS)))
    for by in (1, 2, 4, 8, 16):
        v = v + big * shift_rows(v, by)
        big = big * big
    v = shift_rows(v, 1)
    ubuf[:, 0, :] = v
    ugot[me] = ubuf[me]
    others(send_rows(ubuf, ugot, u_send, u_recv))

    arrived(ntgot, nt_recv)
    total = jnp.sum(ntgot[:, 0, :] + ntgot[:, 1, :] * v, axis=0, keepdims=True) * (1.0 / length)
    rbuf[...] = total
    rgot[mode] = total

    def send_total(i, carry):
        e = half * 16 + lax.rem(mode + i, 16)
        pltpu.make_async_remote_copy(
            rbuf, rgot.at[mode], r_send, r_recv, device_id={"ctx": e}, device_id_type=MESH
        ).start()
        return carry

    lax.fori_loop(1, 16, send_total, 0)

    def within(q, carry):
        s = s_v[q]
        acc = tau[0] * jnp.dot(inner_v[0], s, preferred_element_type=f32)
        for k in range(1, TERMS):
            acc = acc + tau[k] * jnp.dot(inner_v[k], s, preferred_element_type=f32)
        yin[q] = acc
        return carry

    lax.fori_loop(0, steps, within, 0)
    tabs[2].wait()

    arrived(ugot, u_recv)
    for r in range(16):
        u = jnp.concatenate([ugot[r], ugot[16 + r]], axis=1)
        st[r] = cin[r] + p256[r] * u

    for q in reversed(range(steps)):
        levels = [jnp.zeros((8, 256), f32)] * TERMS
        for r in range(16):
            u = st[r]
            for k in range(TERMS):
                levels[k] = levels[k] + fo[k, r : r + 1, :] * u
            st[r] = sq[q, r] + a32_s[r : r + 1, :] * u
        level = jnp.concatenate(levels, axis=0)
        high = level.astype(bf16)
        low = (level - high.astype(f32)).astype(bf16)
        both = jnp.concatenate([high, low], axis=0)
        y = yin[q] + jnp.dot(spread_v[...], both, preferred_element_type=f32)
        out[:, q] = y.astype(bf16).reshape(CHUNKS, WIDTH, 256)

    view = rgot.at[pl.ds(0, 15)]
    pltpu.make_async_copy(view, view, r_recv).wait()
    rgt[:, 0:16] = rgot[:, 0, :].T
    rgrad[...] = rgt[pl.ds(pl.multiple_of(mode * 8, 8), 8), 0:16]

    view = rates.at[pl.ds(0, 8 * (n - 1))]
    pltpu.make_async_copy(view, view, rates_send).wait()
    arrived(sbuf, s_send)
    arrived(ntbuf, nt_send)
    arrived(ubuf, u_send)
    view = rgot.at[pl.ds(0, 15)]
    pltpu.make_async_copy(view, view, r_send).wait()


def local(inner, moment, spread, gate_value, conv_input, output_grad, decay_rate, residue):
    tokens, channels = gate_value.shape
    n = lax.axis_size("ctx")
    steps = tokens // (CHUNKS * WIDTH)
    cut = (CHUNKS, steps, WIDTH, channels)
    V = pltpu.VMEM
    dma = pltpu.SemaphoreType.DMA
    blocks = (steps, CHUNKS, WIDTH, channels)
    size = CHUNKS * WIDTH
    scratch = [
        V(blocks, bf16), V(blocks, bf16), V(blocks, bf16), V((steps, size, channels), bf16),
        V(inner.shape, bf16), V(moment.shape, bf16), V(spread.shape, bf16), V((8, 16), f32), V((8, 16), f32),
        V((8, 128), f32), V((8 * n, 128), f32),
        V((steps, TERMS * CHUNKS, channels), f32), V((steps, TERMS * CHUNKS, channels), f32),
        V((TERMS, 8, channels), f32), V((TERMS, 1, channels), f32),
        V((TERMS, 16, channels), f32), V((TERMS, 16, channels), f32), V((TERMS, 16, channels), f32),
        V((16, channels), f32), V((16, channels), f32), V((16, channels), f32), V((32, 128), f32),
        V((steps, 16, 8, channels), f32), V((16, 8, channels), f32), V((16, 8, channels), f32), V((16, 8, channels), f32),
        V((steps, size, channels), f32),
        V((n, 1, 128), f32), V((n, 2, 128), f32), V((n, 1, 128), f32), V((1, 128), f32),
        V((n, 1, 128), f32), V((n, 2, 128), f32), V((n, 1, 128), f32), V((16, 1, 128), f32), V((128, 128), f32),
        dma((3, steps)), dma((3,)), dma((2,)),
    ] + [dma] * 10
    vmem_spec = pl.BlockSpec(memory_space=pltpu.VMEM)
    hbm_spec = pl.BlockSpec(memory_space=pltpu.HBM)
    out, rgrad = pl.pallas_call(
        functools.partial(kernel, n, tokens * n),
        out_shape=(jax.ShapeDtypeStruct(cut, bf16), jax.ShapeDtypeStruct(residue.shape, f32)),
        in_specs=[hbm_spec] * 8,
        out_specs=(vmem_spec, vmem_spec),
        scratch_shapes=scratch,
        compiler_params=pltpu.CompilerParams(
            collective_id=0, has_side_effects=True, vmem_limit_bytes=24 * 1024 * 1024
        ),
    )(*[
        pltpu.with_memory_space_constraint(a, pltpu.HBM)
        for a in (
            gate_value.reshape(cut), conv_input.reshape(cut), output_grad.reshape(cut),
            decay_rate, residue, inner, moment, spread,
        )
    ])
    return out.reshape(tokens, channels), rgrad


def solution(mesh):
    consts = tables()
    in_specs = (P(), P(), P()) + (P("ctx", "fsdp"),) * 3 + (P(("fsdp", "ctx"), None),) * 2
    out_specs = (P("ctx", "fsdp"), P(("fsdp", "ctx"), None))
    mapped = jax.shard_map(local, mesh=mesh, in_specs=in_specs, out_specs=out_specs, check_vma=False)

    def run(*args):
        return mapped(*[jnp.asarray(c) for c in consts], *args)

    return run
```

```python
import functools
import math

import jax
import jax.numpy as jnp
import numpy as np
from jax import lax
from jax.experimental import pallas as pl
from jax.experimental.pallas import tpu as pltpu
from jax.sharding import PartitionSpec as P

WIDTH = 32
TERMS = 8
CHUNKS = 8
CENTER = (WIDTH - 1) / 2
POINTS = 48
MESH = pl.DeviceIdType.MESH
f32 = jnp.float32
bf16 = jnp.bfloat16


def chebyshev(z):
    rows = [np.ones_like(z), z]
    while len(rows) < TERMS:
        rows.append(2 * z * rows[-1] - rows[-2])
    return np.stack(rows)


def tables(steps):
    i = np.arange(WIDTH)
    basis = chebyshev((i - CENTER) / (WIDTH / 2))
    lag = i[None, :] - i[:, None]
    tri = np.where(lag >= 0, basis[:, np.maximum(lag, 0)], 0.0)
    size = CHUNKS * WIDTH
    inner = np.zeros((TERMS, size, size))
    moment = np.zeros((TERMS, CHUNKS, size))
    for j in range(CHUNKS):
        part = slice(j * WIDTH, (j + 1) * WIDTH)
        inner[:, part, part] = tri
        moment[:, j, part] = basis
    moment = moment.reshape(TERMS * CHUNKS, size)
    spread = np.concatenate([moment.T, moment.T], axis=1)

    total = steps * size
    angle = (2 * np.arange(POINTS) + 1) * math.pi / (2 * POINTS)
    points = (total - 1) / 2 + total / 2 * np.cos(angle)
    order = np.arange(POINTS)
    z = (np.arange(total) - (total - 1) / 2) / (total / 2)
    weight = np.where(order == 0, 1.0, 2.0) / POINTS
    basis = np.cos(np.outer(angle, order)) * weight @ np.cos(np.outer(order, np.arccos(z)))
    basis = basis.reshape(POINTS, CHUNKS, steps, WIDTH).transpose(2, 0, 1, 3).reshape(steps, POINTS, size)
    high = basis.astype(np.float32).astype(jnp.bfloat16)
    low = (basis - high.astype(np.float64)).astype(np.float32).astype(jnp.bfloat16)
    whole = np.concatenate([high, low], axis=1)
    points = np.broadcast_to(points[:, None], (POINTS, 128)).astype(np.float32)
    return [np.asarray(a, np.float32).astype(jnp.bfloat16) for a in (inner, moment, spread)] + [whole, points]


def shift_rows(v, by):
    rows = v.shape[0]
    return jnp.concatenate([v[by:], jnp.zeros((by, v.shape[1]), v.dtype)], axis=0)


def kernel(
    n, length,
    gate, xin, ograd, rate, resid, inner, moment, spread, whole, points,
    out, rgrad,
    g_v, x_v, o_v, s_v, inner_v, moment_v, spread_v, whole_v, points_v, rate_v, resid_v,
    own, pack, rates, m_s, n_s, gacc, tau, en, fx, fo, lam_s, a32_s, a256_s, lamh_s,
    sq, cin, p256, st, yin, stack,
    table, mbuf, mgot, ubuf, ugot, rbuf, rgot,
    in_sem, tab_sem, par_sem,
    rates_send, rates_recv, m_send, m_recv, u_send, u_recv, r_send, r_recv,
):
    me = lax.axis_index("ctx")
    steps = g_v.shape[0]
    chunk = WIDTH * steps
    span = chunk * CHUNKS

    def others(body):
        def step(i, carry):
            body(lax.rem(me + i, n))
            return carry
        lax.fori_loop(1, n, step, 0)

    def put(src, dst, send, recv, e):
        pltpu.make_async_remote_copy(src, dst, send, recv, device_id={"ctx": e}, device_id_type=MESH).start()

    def arrived(view, sem):
        pltpu.make_async_copy(view, view, sem).wait()

    barrier = pltpu.get_barrier_semaphore()
    others(lambda e: pl.semaphore_signal(barrier, inc=1, device_id={"ctx": e}, device_id_type=MESH))

    par = [pltpu.make_async_copy(rate, rate_v, par_sem.at[0]), pltpu.make_async_copy(resid, resid_v, par_sem.at[1])]
    for c in par:
        c.start()
    tabs = [
        pltpu.make_async_copy(src, dst, tab_sem.at[k])
        for k, (src, dst) in enumerate((
            (whole, whole_v), (points, points_v), (moment, moment_v), (inner, inner_v), (spread, spread_v)
        ))
    ]

    arrays = ((gate, g_v), (ograd, o_v), (xin, x_v))

    def fetch(q, which):
        return [
            pltpu.make_async_copy(arrays[k][0].at[:, q], arrays[k][1].at[q], in_sem.at[k, q]) for k in which
        ]

    for c in fetch(0, (0, 1)):
        c.start()
    tabs[0].start()
    for q in range(1, steps):
        for c in fetch(q, (0, 1)):
            c.start()
    for c in tabs[1:4]:
        c.start()
    for q in range(steps):
        fetch(q, (2,))[0].start()
    tabs[4].start()

    own[...] = jnp.zeros_like(own)
    stack[...] = jnp.zeros_like(stack)
    for c in par:
        c.wait()
    own[0, :, 0:16] = rate_v[...]
    own[1, :, 0:16] = resid_v[...]
    for i in range(2):
        row = own[i, 0:1]
        for c in range(1, 8):
            row = row + pltpu.roll(own[i, c : c + 1], 128 - 16 * c, 1)
        pack[i : i + 1] = row
    row = own[0, 0:1]
    for c in range(1, 8):
        row = row + pltpu.roll(own[0, c : c + 1], 16 * c, 1)
    rates[me] = pack[...]

    lane = lax.broadcasted_iota(jnp.int32, (8, 128), 1)
    group, place = lane // 16, lax.broadcasted_iota(jnp.int32, (8, 128), 0)

    def to_rows(block, count, dst):
        turned = block.T
        for e in range(n):
            tile = pltpu.roll(turned[8 * e : 8 * e + 8], 0, 1, stride=16, stride_axis=0)
            for i in range(count):
                line = jnp.sum(jnp.where(group == (place + i) % 8, tile, 0.0), axis=0, keepdims=True)
                dst[e, i : i + 1] = line if i == 0 else pltpu.roll(line, 128 - 16 * i, 1)

    tabs[0].wait()
    for q in range(steps):
        for c in fetch(q, (0, 1)):
            c.wait()
        s = (o_v[q].astype(f32) * g_v[q].astype(f32)).astype(bf16).reshape(256, 256)
        s_v[q] = s
        part = jnp.dot(whole_v[q], s, preferred_element_type=f32)
        sums = part if q == 0 else sums + part
    stack[0:POINTS] = sums[0:POINTS] + sums[POINTS:]
    to_rows(stack[...], POINTS // 16, mbuf)
    mgot[me] = mbuf[me]

    tabs[1].wait()
    falls = jnp.exp(points_v[...] * (-row))
    square = (128, 128)
    same = lax.broadcasted_iota(jnp.int32, square, 0) // 16 == lax.broadcasted_iota(jnp.int32, square, 1) // 16
    for i in range(POINTS // 16):
        part = jnp.concatenate([falls[16 * i : 16 * i + 16]] * 8, axis=0)
        table[128 * i : 128 * i + 128] = jnp.where(same, part, 0.0)

    pl.semaphore_wait(barrier, n - 1)
    others(lambda e: put(mbuf.at[e], mgot.at[me], m_send, m_recv, e))
    others(lambda e: put(pack, rates.at[me], rates_send, rates_recv, e))

    for k in range(TERMS):
        gacc[k] = jnp.zeros_like(gacc[k])
    tabs[2].wait()
    tabs[3].wait()

    def first(q, carry):
        fetch(q, (2,))[0].wait()
        s = s_v[q]
        x = x_v[q].reshape(256, 256)
        m_s[q] = jnp.dot(moment_v[...], s, preferred_element_type=f32)
        n_s[q] = jnp.dot(moment_v[...], x, preferred_element_type=f32)
        wide = x.astype(f32)
        for k in range(TERMS):
            near = jnp.dot(inner_v[k], s, preferred_element_type=f32)
            gacc[k] += jnp.sum((near * wide).reshape(32, 8, 256), axis=0)
        return carry

    lax.fori_loop(0, steps, first, 0)

    arrived(mgot.at[pl.ds(0, n - 1)], m_recv)
    sums = jnp.concatenate([mgot[:, i, :] for i in range(POINTS // 16)], axis=1)
    v = jnp.dot(sums, table[...], precision=lax.Precision.HIGHEST, preferred_element_type=f32)
    big = jnp.exp(row * (-float(span)))
    for by in (1, 2, 4, 8, 16):
        v = v + big * shift_rows(v, by)
        big = big * big
    states = shift_rows(v, 1)
    wide_group = lax.broadcasted_iota(jnp.int32, (n, 128), 1) // 16
    mirrored = states
    for c in range(1, 8):
        mirrored = jnp.where(wide_group == 8 - c, pltpu.roll(states, (128 - 32 * c) % 128, 1), mirrored)
    ubuf[:, 0, :] = mirrored
    ugot[me] = ubuf[me]
    others(lambda e: put(ubuf.at[e], ugot.at[me], u_send, u_recv, e))

    arrived(rates.at[pl.ds(0, n - 1)], rates_recv)
    tiles = []
    for e in range(n):
        a = pltpu.roll(jnp.broadcast_to(rates[e, 0:1], (8, 128)), 0, 1, stride=16, stride_axis=0)
        b = pltpu.roll(jnp.broadcast_to(rates[e, 1:2], (8, 128)), 16, 1, stride=16, stride_axis=0)
        tiles.append(jnp.where(lane < 16, a, b))
    turned = jnp.concatenate(tiles, axis=0).T
    lam, res = turned[0:16], turned[16:32]
    lam_s[...] = lam
    lamh_s[0:16] = lam[:, 0:128]
    lamh_s[16:32] = lam[:, 128:256]
    a32_s[...] = jnp.exp(-WIDTH * lam)
    a256_s[...] = jnp.exp(-chunk * lam)
    ahead = jnp.exp(-CENTER * lam)
    behind = jnp.exp(-(WIDTH - CENTER) * lam)
    h = lam * (WIDTH / 4)
    w = h * h
    power = jnp.ones_like(h)
    for k in range(TERMS):
        tail = 1.0 + w * (1.0 / (4 * (k + 4)))
        for m in (3, 2, 1):
            tail = 1.0 + w * tail * (1.0 / (m * (k + m)))
        term = power * tail * ((1.0 if k == 0 else 2.0) / math.factorial(k))
        e = ahead * (term if k % 2 == 0 else -term)
        b = behind * term
        en[k] = e
        fx[k] = b
        fo[k] = b * res
        tau[k] = jnp.sum(e * res, axis=0, keepdims=True)
        power = power * h

    def scan(r, carry):
        row = pl.ds(r, 1)
        e = [en[k, row, :] for k in range(TERMS)]
        a = a32_s[row, :]
        u = None
        for q in reversed(range(steps)):
            new = e[0] * m_s[q, 0:8]
            for k in range(1, TERMS):
                new = new + e[k] * m_s[q, 8 * k : 8 * k + 8]
            sq[q, r] = new
            u = new if u is None else new + a * u
        big = a256_s[row, :]
        for by in (1, 2, 4):
            u = u + big * shift_rows(u, by)
            big = big * big
        cin[r] = shift_rows(u, 1)
        return carry

    lax.fori_loop(0, 16, scan, 0, unroll=2)

    behind_chunks = (7 - lax.broadcasted_iota(jnp.int32, (8, 256), 0)).astype(f32) * (-float(chunk))
    gsum = [jnp.sum(gacc[k], axis=0, keepdims=True) for k in range(TERMS)]

    def share(r, carry):
        row = pl.ds(r, 1)
        f = [fx[k, row, :] for k in range(TERMS)]
        a = a32_s[row, :]
        reach = jnp.exp(behind_chunks * lam_s[row, :])
        p256[r] = reach
        u = cin[r]
        acc = jnp.zeros((8, 256), f32)
        tail = jnp.zeros((8, 256), f32)
        fall = jnp.ones((1, 256), f32)
        for q in reversed(range(steps)):
            v = f[0] * n_s[q, 0:8]
            for k in range(1, TERMS):
                v = v + f[k] * n_s[q, 8 * k : 8 * k + 8]
            acc = acc + v * u
            tail = tail + v * fall
            if q:
                u = sq[q, r] + a * u
                fall = fall * a
        near = jnp.sum(acc, axis=0, keepdims=True)
        for k in range(TERMS):
            near = near + en[k, row, :] * gsum[k]
        stack[row] = near
        stack[pl.ds(16 + r, 1)] = jnp.sum(tail * reach, axis=0, keepdims=True)
        return carry

    lax.fori_loop(0, 16, share, 0, unroll=2)

    to_rows(stack[...], 2, rbuf)
    rgot[me] = rbuf[me]
    others(lambda e: put(rbuf.at[e], rgot.at[me], r_send, r_recv, e))

    def within(q, carry):
        s = s_v[q]
        acc = tau[0] * jnp.dot(inner_v[0], s, preferred_element_type=f32)
        for k in range(1, TERMS):
            acc = acc + tau[k] * jnp.dot(inner_v[k], s, preferred_element_type=f32)
        yin[q] = acc
        return carry

    lax.fori_loop(0, steps, within, 0)
    tabs[4].wait()

    arrived(ugot.at[pl.ds(0, n - 1)], u_recv)
    tiles = [
        pltpu.roll(jnp.broadcast_to(ugot[e], (8, 128)), 0, 1, stride=16, stride_axis=0) for e in range(n)
    ]
    turned = jnp.concatenate(tiles, axis=0).T
    for r in range(16):
        st[r] = cin[r] + p256[r] * turned[r : r + 1]

    for q in reversed(range(steps)):
        levels = [jnp.zeros((8, 256), f32)] * TERMS
        for r in range(16):
            u = st[r]
            for k in range(TERMS):
                levels[k] = levels[k] + fo[k, r : r + 1, :] * u
            if q:
                st[r] = sq[q, r] + a32_s[r : r + 1, :] * u
        level = jnp.concatenate(levels, axis=0)
        high = level.astype(bf16)
        low = (level - high.astype(f32)).astype(bf16)
        both = jnp.concatenate([high, low], axis=0)
        y = yin[q] + jnp.dot(spread_v[...], both, preferred_element_type=f32)
        out[:, q] = y.astype(bf16).reshape(CHUNKS, WIDTH, 256)

    arrived(rgot.at[pl.ds(0, n - 1)], r_recv)
    total = jnp.sum(rgot[:, 0, :] + rgot[:, 1, :] * states, axis=0, keepdims=True)
    total = total * (1.0 / length)
    for c in range(8):
        moved = total if c == 0 else pltpu.roll(total, 128 - 16 * c, 1)
        rgrad[c : c + 1] = moved[:, 0:16]

    arrived(rates.at[pl.ds(0, n - 1)], rates_send)
    arrived(mgot.at[pl.ds(0, n - 1)], m_send)
    arrived(ugot.at[pl.ds(0, n - 1)], u_send)
    arrived(rgot.at[pl.ds(0, n - 1)], r_send)


def local(inner, moment, spread, whole, points, gate_value, conv_input, output_grad, decay_rate, residue):
    tokens, channels = gate_value.shape
    n = lax.axis_size("ctx")
    steps = tokens // (CHUNKS * WIDTH)
    cut = (CHUNKS, steps, WIDTH, channels)
    V = pltpu.VMEM
    dma = pltpu.SemaphoreType.DMA
    blocks = (steps, CHUNKS, WIDTH, channels)
    size = CHUNKS * WIDTH
    scratch = [
        V(blocks, bf16), V(blocks, bf16), V(blocks, bf16), V((steps, size, channels), bf16),
        V(inner.shape, bf16), V(moment.shape, bf16), V(spread.shape, bf16), V(whole.shape, bf16), V(points.shape, f32), V((8, 16), f32), V((8, 16), f32),
        V((2, 8, 128), f32), V((2, 128), f32), V((n, 2, 128), f32),
        V((steps, TERMS * CHUNKS, channels), f32), V((steps, TERMS * CHUNKS, channels), f32),
        V((TERMS, 8, channels), f32), V((TERMS, 1, channels), f32),
        V((TERMS, 16, channels), f32), V((TERMS, 16, channels), f32), V((TERMS, 16, channels), f32),
        V((16, channels), f32), V((16, channels), f32), V((16, channels), f32), V((32, 128), f32),
        V((steps, 16, 8, channels), f32), V((16, 8, channels), f32), V((16, 8, channels), f32), V((16, 8, channels), f32),
        V((steps, size, channels), f32), V((128, channels), f32),
        V((8 * POINTS, 128), f32), V((n, POINTS // 16, 128), f32), V((n, POINTS // 16, 128), f32),
        V((n, 1, 128), f32), V((n, 1, 128), f32), V((n, 2, 128), f32), V((n, 2, 128), f32),
        dma((3, steps)), dma((5,)), dma((2,)),
    ] + [dma] * 8
    vmem_spec = pl.BlockSpec(memory_space=pltpu.VMEM)
    hbm_spec = pl.BlockSpec(memory_space=pltpu.HBM)
    out, rgrad = pl.pallas_call(
        functools.partial(kernel, n, tokens * n),
        out_shape=(jax.ShapeDtypeStruct(cut, bf16), jax.ShapeDtypeStruct(residue.shape, f32)),
        in_specs=[hbm_spec] * 10,
        out_specs=(vmem_spec, vmem_spec),
        scratch_shapes=scratch,
        compiler_params=pltpu.CompilerParams(
            collective_id=0, has_side_effects=True, vmem_limit_bytes=24 * 1024 * 1024
        ),
    )(*[
        pltpu.with_memory_space_constraint(a, pltpu.HBM)
        for a in (
            gate_value.reshape(cut), conv_input.reshape(cut), output_grad.reshape(cut),
            decay_rate, residue, inner, moment, spread, whole, points,
        )
    ])
    return out.reshape(tokens, channels), rgrad


def solution(mesh):
    consts = tables(8)
    in_specs = (P(),) * 5 + (P("ctx", "fsdp"),) * 3 + (P(("fsdp", "ctx"), None),) * 2
    out_specs = (P("ctx", "fsdp"), P(("fsdp", "ctx"), None))
    mapped = jax.shard_map(local, mesh=mesh, in_specs=in_specs, out_specs=out_specs, check_vma=False)

    def run(*args):
        return mapped(*[jnp.asarray(c) for c in consts], *args)

    return run
```

```python
import functools
import math

import jax
import jax.numpy as jnp
import numpy as np
from jax import lax
from jax.experimental import pallas as pl
from jax.experimental.pallas import tpu as pltpu
from jax.sharding import PartitionSpec as P

WIDTH = 32
TERMS = 8
CHUNKS = 8
CENTER = (WIDTH - 1) / 2
POINTS = 48
MESH = pl.DeviceIdType.MESH
f32 = jnp.float32
bf16 = jnp.bfloat16


def chebyshev(z):
    rows = [np.ones_like(z), z]
    while len(rows) < TERMS:
        rows.append(2 * z * rows[-1] - rows[-2])
    return np.stack(rows)


def tables(steps):
    i = np.arange(WIDTH)
    basis = chebyshev((i - CENTER) / (WIDTH / 2))
    lag = i[None, :] - i[:, None]
    tri = np.where(lag >= 0, basis[:, np.maximum(lag, 0)], 0.0)
    size = CHUNKS * WIDTH
    inner = np.zeros((TERMS, size, size))
    moment = np.zeros((TERMS, CHUNKS, size))
    for j in range(CHUNKS):
        part = slice(j * WIDTH, (j + 1) * WIDTH)
        inner[:, part, part] = tri
        moment[:, j, part] = basis
    moment = moment.reshape(TERMS * CHUNKS, size)
    spread = np.concatenate([moment.T, moment.T], axis=1)

    total = steps * size
    angle = (2 * np.arange(POINTS) + 1) * math.pi / (2 * POINTS)
    points = (total - 1) / 2 + total / 2 * np.cos(angle)
    order = np.arange(POINTS)
    z = (np.arange(total) - (total - 1) / 2) / (total / 2)
    weight = np.where(order == 0, 1.0, 2.0) / POINTS
    basis = np.cos(np.outer(angle, order)) * weight @ np.cos(np.outer(order, np.arccos(z)))
    basis = basis.reshape(POINTS, CHUNKS, steps, WIDTH).transpose(2, 0, 1, 3).reshape(steps, POINTS, size)
    high = basis.astype(np.float32).astype(jnp.bfloat16)
    low = (basis - high.astype(np.float64)).astype(np.float32).astype(jnp.bfloat16)
    whole = np.concatenate([high, low], axis=1)
    points = np.broadcast_to(points[:, None], (POINTS, 128)).astype(np.float32)
    return [np.asarray(a, np.float32).astype(jnp.bfloat16) for a in (inner, moment, spread)] + [whole, points]


def shift_rows(v, by):
    rows = v.shape[0]
    return jnp.concatenate([v[by:], jnp.zeros((by, v.shape[1]), v.dtype)], axis=0)


def kernel(
    n, length,
    gate, xin, ograd, rate, resid, inner, moment, spread, whole, points,
    out, rgrad,
    g_v, x_v, o_v, s_v, inner_v, moment_v, spread_v, whole_v, points_v, rate_v, resid_v,
    own, pack, rates, m_s, n_s, gacc, tau, en, fx, fo, lam_s, a32_s, a256_s, lamh_s,
    sq, cin, p256, st, yin, stack,
    table, mbuf, mgot, ubuf, ugot, rbuf, rgot,
    in_sem, tab_sem, par_sem,
    rates_send, rates_recv, m_send, m_recv, u_send, u_recv, r_send, r_recv,
):
    me = lax.axis_index("ctx")
    steps = g_v.shape[0]
    chunk = WIDTH * steps
    span = chunk * CHUNKS

    def others(body):
        def step(i, carry):
            body(lax.rem(me + i, n))
            return carry
        lax.fori_loop(1, n, step, 0)

    def put(src, dst, send, recv, e):
        pltpu.make_async_remote_copy(src, dst, send, recv, device_id={"ctx": e}, device_id_type=MESH).start()

    def arrived(view, sem):
        pltpu.make_async_copy(view, view, sem).wait()

    barrier = pltpu.get_barrier_semaphore()
    others(lambda e: pl.semaphore_signal(barrier, inc=1, device_id={"ctx": e}, device_id_type=MESH))

    par = [pltpu.make_async_copy(rate, rate_v, par_sem.at[0]), pltpu.make_async_copy(resid, resid_v, par_sem.at[1])]
    for c in par:
        c.start()
    tabs = [
        pltpu.make_async_copy(src, dst, tab_sem.at[k])
        for k, (src, dst) in enumerate((
            (whole, whole_v), (points, points_v), (moment, moment_v), (inner, inner_v), (spread, spread_v)
        ))
    ]

    arrays = ((gate, g_v), (ograd, o_v), (xin, x_v))

    def fetch(q, which):
        return [
            pltpu.make_async_copy(arrays[k][0].at[:, q], arrays[k][1].at[q], in_sem.at[k, q]) for k in which
        ]

    for c in fetch(0, (0, 1)):
        c.start()
    tabs[0].start()
    for q in range(1, steps):
        for c in fetch(q, (0, 1)):
            c.start()
    for c in tabs[1:4]:
        c.start()
    for q in range(steps):
        fetch(q, (2,))[0].start()
    tabs[4].start()

    own[...] = jnp.zeros_like(own)
    stack[...] = jnp.zeros_like(stack)
    for c in par:
        c.wait()
    own[0, :, 0:16] = rate_v[...]
    own[1, :, 0:16] = resid_v[...]
    for i in range(2):
        row = own[i, 0:1]
        for c in range(1, 8):
            row = row + pltpu.roll(own[i, c : c + 1], 128 - 16 * c, 1)
        pack[i : i + 1] = row
    row = own[0, 0:1]
    for c in range(1, 8):
        row = row + pltpu.roll(own[0, c : c + 1], 16 * c, 1)
    rates[me] = pack[...]

    lane = lax.broadcasted_iota(jnp.int32, (8, 128), 1)
    group, place = lane // 16, lax.broadcasted_iota(jnp.int32, (8, 128), 0)

    def to_rows(block, count, dst):
        turned = block.T
        for e in range(n):
            tile = pltpu.roll(turned[8 * e : 8 * e + 8], 0, 1, stride=16, stride_axis=0)
            for i in range(count):
                line = jnp.sum(jnp.where(group == (place + i) % 8, tile, 0.0), axis=0, keepdims=True)
                dst[e, i : i + 1] = line if i == 0 else pltpu.roll(line, 128 - 16 * i, 1)

    tabs[0].wait()
    for q in range(steps):
        for c in fetch(q, (0, 1)):
            c.wait()
        s = (o_v[q].astype(f32) * g_v[q].astype(f32)).astype(bf16).reshape(256, 256)
        s_v[q] = s
        part = jnp.dot(whole_v[q], s, preferred_element_type=f32)
        sums = part if q == 0 else sums + part
    stack[0:POINTS] = sums[0:POINTS] + sums[POINTS:]
    to_rows(stack[...], POINTS // 16, mbuf)
    mgot[me] = mbuf[me]

    tabs[1].wait()
    falls = jnp.exp(points_v[...] * (-row))
    square = (128, 128)
    same = lax.broadcasted_iota(jnp.int32, square, 0) // 16 == lax.broadcasted_iota(jnp.int32, square, 1) // 16
    for i in range(POINTS // 16):
        part = jnp.concatenate([falls[16 * i : 16 * i + 16]] * 8, axis=0)
        table[128 * i : 128 * i + 128] = jnp.where(same, part, 0.0)

    pl.semaphore_wait(barrier, n - 1)
    others(lambda e: put(mbuf.at[e], mgot.at[me], m_send, m_recv, e))
    others(lambda e: put(pack, rates.at[me], rates_send, rates_recv, e))

    for k in range(TERMS):
        gacc[k] = jnp.zeros_like(gacc[k])
    tabs[2].wait()
    tabs[3].wait()

    def first(q, carry):
        fetch(q, (2,))[0].wait()
        s = s_v[q]
        x = x_v[q].reshape(256, 256)
        m_s[q] = jnp.dot(moment_v[...], s, preferred_element_type=f32)
        n_s[q] = jnp.dot(moment_v[...], x, preferred_element_type=f32)
        wide = x.astype(f32)
        for k in range(TERMS):
            near = jnp.dot(inner_v[k], s, preferred_element_type=f32)
            gacc[k] += jnp.sum((near * wide).reshape(32, 8, 256), axis=0)
        return carry

    lax.fori_loop(0, steps, first, 0)

    arrived(mgot.at[pl.ds(0, n - 1)], m_recv)
    sums = jnp.concatenate([mgot[:, i, :] for i in range(POINTS // 16)], axis=1)
    v = jnp.dot(sums, table[...], precision=lax.Precision.HIGHEST, preferred_element_type=f32)
    big = jnp.exp(row * (-float(span)))
    for by in (1, 2, 4, 8, 16):
        v = v + big * shift_rows(v, by)
        big = big * big
    states = shift_rows(v, 1)
    wide_group = lax.broadcasted_iota(jnp.int32, (n, 128), 1) // 16
    mirrored = states
    for c in range(1, 8):
        mirrored = jnp.where(wide_group == 8 - c, pltpu.roll(states, (128 - 32 * c) % 128, 1), mirrored)
    ubuf[:, 0, :] = mirrored
    ugot[me] = ubuf[me]
    others(lambda e: put(ubuf.at[e], ugot.at[me], u_send, u_recv, e))

    arrived(rates.at[pl.ds(0, n - 1)], rates_recv)
    tiles = []
    for e in range(n):
        a = pltpu.roll(jnp.broadcast_to(rates[e, 0:1], (8, 128)), 0, 1, stride=16, stride_axis=0)
        b = pltpu.roll(jnp.broadcast_to(rates[e, 1:2], (8, 128)), 16, 1, stride=16, stride_axis=0)
        tiles.append(jnp.where(lane < 16, a, b))
    turned = jnp.concatenate(tiles, axis=0).T
    lam, res = turned[0:16], turned[16:32]
    lam_s[...] = lam
    lamh_s[0:16] = lam[:, 0:128]
    lamh_s[16:32] = lam[:, 128:256]
    a32_s[...] = jnp.exp(-WIDTH * lam)
    a256_s[...] = jnp.exp(-chunk * lam)
    ahead = jnp.exp(-CENTER * lam)
    behind = jnp.exp(-(WIDTH - CENTER) * lam)
    h = lam * (WIDTH / 4)
    w = h * h
    power = jnp.ones_like(h)
    for k in range(TERMS):
        tail = 1.0 + w * (1.0 / (4 * (k + 4)))
        for m in (3, 2, 1):
            tail = 1.0 + w * tail * (1.0 / (m * (k + m)))
        term = power * tail * ((1.0 if k == 0 else 2.0) / math.factorial(k))
        e = ahead * (term if k % 2 == 0 else -term)
        b = behind * term
        en[k] = e
        fx[k] = b
        fo[k] = b * res
        tau[k] = jnp.sum(e * res, axis=0, keepdims=True)
        power = power * h

    def scan(r, carry):
        row = pl.ds(r, 1)
        e = [en[k, row, :] for k in range(TERMS)]
        a = a32_s[row, :]
        u = None
        for q in reversed(range(steps)):
            new = e[0] * m_s[q, 0:8]
            for k in range(1, TERMS):
                new = new + e[k] * m_s[q, 8 * k : 8 * k + 8]
            sq[q, r] = new
            u = new if u is None else new + a * u
        big = a256_s[row, :]
        for by in (1, 2, 4):
            u = u + big * shift_rows(u, by)
            big = big * big
        cin[r] = shift_rows(u, 1)
        return carry

    lax.fori_loop(0, 16, scan, 0, unroll=2)

    behind_chunks = (7 - lax.broadcasted_iota(jnp.int32, (8, 256), 0)).astype(f32) * (-float(chunk))
    gsum = [jnp.sum(gacc[k], axis=0, keepdims=True) for k in range(TERMS)]

    def share(r, carry):
        row = pl.ds(r, 1)
        f = [fx[k, row, :] for k in range(TERMS)]
        a = a32_s[row, :]
        reach = jnp.exp(behind_chunks * lam_s[row, :])
        p256[r] = reach
        u = cin[r]
        acc = jnp.zeros((8, 256), f32)
        tail = jnp.zeros((8, 256), f32)
        fall = jnp.ones((1, 256), f32)
        for q in reversed(range(steps)):
            v = f[0] * n_s[q, 0:8]
            for k in range(1, TERMS):
                v = v + f[k] * n_s[q, 8 * k : 8 * k + 8]
            acc = acc + v * u
            tail = tail + v * fall
            if q:
                u = sq[q, r] + a * u
                fall = fall * a
        near = jnp.sum(acc, axis=0, keepdims=True)
        for k in range(TERMS):
            near = near + en[k, row, :] * gsum[k]
        stack[row] = near
        stack[pl.ds(16 + r, 1)] = jnp.sum(tail * reach, axis=0, keepdims=True)
        return carry

    lax.fori_loop(0, 16, share, 0, unroll=2)

    to_rows(stack[...], 2, rbuf)
    rgot[me] = rbuf[me]
    others(lambda e: put(rbuf.at[e], rgot.at[me], r_send, r_recv, e))

    def within(q, carry):
        s = s_v[q]
        acc = tau[0] * jnp.dot(inner_v[0], s, preferred_element_type=f32)
        for k in range(1, TERMS):
            acc = acc + tau[k] * jnp.dot(inner_v[k], s, preferred_element_type=f32)
        yin[q] = acc
        return carry

    lax.fori_loop(0, steps, within, 0)
    tabs[4].wait()

    arrived(ugot.at[pl.ds(0, n - 1)], u_recv)
    tiles = [
        pltpu.roll(jnp.broadcast_to(ugot[e], (8, 128)), 0, 1, stride=16, stride_axis=0) for e in range(n)
    ]
    turned = jnp.concatenate(tiles, axis=0).T
    for r in range(16):
        st[r] = cin[r] + p256[r] * turned[r : r + 1]

    for q in reversed(range(steps)):
        levels = [jnp.zeros((8, 256), f32)] * TERMS
        for r in range(16):
            u = st[r]
            for k in range(TERMS):
                levels[k] = levels[k] + fo[k, r : r + 1, :] * u
            if q:
                st[r] = sq[q, r] + a32_s[r : r + 1, :] * u
        level = jnp.concatenate(levels, axis=0)
        high = level.astype(bf16)
        low = (level - high.astype(f32)).astype(bf16)
        both = jnp.concatenate([high, low], axis=0)
        y = yin[q] + jnp.dot(spread_v[...], both, preferred_element_type=f32)
        out[:, q] = y.astype(bf16).reshape(CHUNKS, WIDTH, 256)

    arrived(rgot.at[pl.ds(0, n - 1)], r_recv)
    total = jnp.sum(rgot[:, 0, :] + rgot[:, 1, :] * states, axis=0, keepdims=True)
    total = total * (1.0 / length)
    for c in range(8):
        moved = total if c == 0 else pltpu.roll(total, 128 - 16 * c, 1)
        rgrad[c : c + 1] = moved[:, 0:16]

    arrived(rates.at[pl.ds(0, n - 1)], rates_send)
    arrived(mgot.at[pl.ds(0, n - 1)], m_send)
    arrived(ugot.at[pl.ds(0, n - 1)], u_send)
    arrived(rgot.at[pl.ds(0, n - 1)], r_send)


def store(y, r, out, rgrad, sems):
    parts = y.shape[0]
    copies = [pltpu.make_async_copy(r, rgrad, sems.at[parts])]
    copies += [pltpu.make_async_copy(y.at[j], out.at[j], sems.at[j]) for j in range(parts)]
    for c in copies:
        c.start()
    for c in copies:
        c.wait()


def local(inner, moment, spread, whole, points, gate_value, conv_input, output_grad, decay_rate, residue):
    tokens, channels = gate_value.shape
    n = lax.axis_size("ctx")
    steps = tokens // (CHUNKS * WIDTH)
    cut = (CHUNKS, steps, WIDTH, channels)
    V = pltpu.VMEM
    dma = pltpu.SemaphoreType.DMA
    blocks = (steps, CHUNKS, WIDTH, channels)
    size = CHUNKS * WIDTH
    scratch = [
        V(blocks, bf16), V(blocks, bf16), V(blocks, bf16), V((steps, size, channels), bf16),
        V(inner.shape, bf16), V(moment.shape, bf16), V(spread.shape, bf16), V(whole.shape, bf16), V(points.shape, f32), V((8, 16), f32), V((8, 16), f32),
        V((2, 8, 128), f32), V((2, 128), f32), V((n, 2, 128), f32),
        V((steps, TERMS * CHUNKS, channels), f32), V((steps, TERMS * CHUNKS, channels), f32),
        V((TERMS, 8, channels), f32), V((TERMS, 1, channels), f32),
        V((TERMS, 16, channels), f32), V((TERMS, 16, channels), f32), V((TERMS, 16, channels), f32),
        V((16, channels), f32), V((16, channels), f32), V((16, channels), f32), V((32, 128), f32),
        V((steps, 16, 8, channels), f32), V((16, 8, channels), f32), V((16, 8, channels), f32), V((16, 8, channels), f32),
        V((steps, size, channels), f32), V((128, channels), f32),
        V((8 * POINTS, 128), f32), V((n, POINTS // 16, 128), f32), V((n, POINTS // 16, 128), f32),
        V((n, 1, 128), f32), V((n, 1, 128), f32), V((n, 2, 128), f32), V((n, 2, 128), f32),
        dma((3, steps)), dma((5,)), dma((2,)),
    ] + [dma] * 8
    vmem_spec = pl.BlockSpec(memory_space=pltpu.VMEM)
    hbm_spec = pl.BlockSpec(memory_space=pltpu.HBM)
    out, rgrad = pl.pallas_call(
        functools.partial(kernel, n, tokens * n),
        out_shape=(jax.ShapeDtypeStruct(cut, bf16), jax.ShapeDtypeStruct(residue.shape, f32)),
        in_specs=[hbm_spec] * 10,
        out_specs=(vmem_spec, vmem_spec),
        scratch_shapes=scratch,
        compiler_params=pltpu.CompilerParams(
            collective_id=0, has_side_effects=True, vmem_limit_bytes=24 * 1024 * 1024
        ),
    )(*[
        pltpu.with_memory_space_constraint(a, pltpu.HBM)
        for a in (
            gate_value.reshape(cut), conv_input.reshape(cut), output_grad.reshape(cut),
            decay_rate, residue, inner, moment, spread, whole, points,
        )
    ])
    out, rgrad = pl.pallas_call(
        store,
        out_shape=(jax.ShapeDtypeStruct(cut, bf16), jax.ShapeDtypeStruct(residue.shape, f32)),
        in_specs=[vmem_spec] * 2,
        out_specs=(hbm_spec, hbm_spec),
        scratch_shapes=[dma((CHUNKS + 1,))],
    )(*[pltpu.with_memory_space_constraint(a, pltpu.VMEM) for a in (out, rgrad)])
    return out.reshape(tokens, channels), rgrad


def solution(mesh):
    consts = tables(8)
    in_specs = (P(),) * 5 + (P("ctx", "fsdp"),) * 3 + (P(("fsdp", "ctx"), None),) * 2
    out_specs = (P("ctx", "fsdp"), P(("fsdp", "ctx"), None))
    mapped = jax.shard_map(local, mesh=mesh, in_specs=in_specs, out_specs=out_specs, check_vma=False)

    def run(*args):
        return mapped(*[jnp.asarray(c) for c in consts], *args)

    return run
```

```python
import functools
import math

import jax
import jax.numpy as jnp
import numpy as np
from jax import lax
from jax.experimental import pallas as pl
from jax.experimental.pallas import tpu as pltpu
from jax.sharding import PartitionSpec as P

WIDTH = 32
TERMS = 8
CHUNKS = 8
CENTER = (WIDTH - 1) / 2
POINTS = 48
MESH = pl.DeviceIdType.MESH
f32 = jnp.float32
bf16 = jnp.bfloat16


def chebyshev(z):
    rows = [np.ones_like(z), z]
    while len(rows) < TERMS:
        rows.append(2 * z * rows[-1] - rows[-2])
    return np.stack(rows)


def tables(steps):
    i = np.arange(WIDTH)
    basis = chebyshev((i - CENTER) / (WIDTH / 2))
    lag = i[None, :] - i[:, None]
    tri = np.where(lag >= 0, basis[:, np.maximum(lag, 0)], 0.0)
    size = CHUNKS * WIDTH
    inner = np.zeros((TERMS, size, size))
    moment = np.zeros((TERMS, CHUNKS, size))
    for j in range(CHUNKS):
        part = slice(j * WIDTH, (j + 1) * WIDTH)
        inner[:, part, part] = tri
        moment[:, j, part] = basis
    moment = moment.reshape(TERMS * CHUNKS, size)
    spread = np.concatenate([moment.T, moment.T], axis=1)

    total = steps * size
    angle = (2 * np.arange(POINTS) + 1) * math.pi / (2 * POINTS)
    points = (total - 1) / 2 + total / 2 * np.cos(angle)
    order = np.arange(POINTS)
    z = (np.arange(total) - (total - 1) / 2) / (total / 2)
    weight = np.where(order == 0, 1.0, 2.0) / POINTS
    basis = np.cos(np.outer(angle, order)) * weight @ np.cos(np.outer(order, np.arccos(z)))
    basis = basis.reshape(POINTS, CHUNKS, steps, WIDTH).transpose(2, 0, 1, 3).reshape(steps, POINTS, size)
    high = basis.astype(np.float32).astype(jnp.bfloat16)
    low = (basis - high.astype(np.float64)).astype(np.float32).astype(jnp.bfloat16)
    whole = np.concatenate([high, low], axis=1)
    points = np.broadcast_to(points[:, None], (POINTS, 128)).astype(np.float32)
    return [np.asarray(a, np.float32).astype(jnp.bfloat16) for a in (inner, moment, spread)] + [whole, points]


def shift_rows(v, by):
    rows = v.shape[0]
    return jnp.concatenate([v[by:], jnp.zeros((by, v.shape[1]), v.dtype)], axis=0)


def kernel(
    n, length,
    gate, xin, ograd, rate, resid, inner, moment, spread, whole, points,
    out, rgrad,
    g_v, x_v, o_v, s_v, inner_v, moment_v, spread_v, whole_v, points_v, rate_v, resid_v,
    own, pack, rates, m_s, n_s, gacc, tau, en, fx, fo, lam_s, a32_s, a256_s, lamh_s,
    sq, cin, p256, st, yin, stack,
    table, mbuf, mgot, ubuf, ugot, rbuf, rgot,
    in_sem, tab_sem, par_sem,
    rates_send, rates_recv, m_send, m_recv, u_send, u_recv, r_send, r_recv,
):
    me = lax.axis_index("ctx")
    steps = g_v.shape[0]
    chunk = WIDTH * steps
    span = chunk * CHUNKS

    order = sorted(range(1, n), key=lambda i: -(min(i // 2 % 8, 8 - i // 2 % 8) + i // 16))

    def others(body):
        for i in order:
            body(lax.rem(me + i, n))

    def put(src, dst, send, recv, e):
        pltpu.make_async_remote_copy(src, dst, send, recv, device_id={"ctx": e}, device_id_type=MESH).start()

    def arrived(view, sem):
        pltpu.make_async_copy(view, view, sem).wait()

    barrier = pltpu.get_barrier_semaphore()
    others(lambda e: pl.semaphore_signal(barrier, inc=1, device_id={"ctx": e}, device_id_type=MESH))

    par = [pltpu.make_async_copy(rate, rate_v, par_sem.at[0]), pltpu.make_async_copy(resid, resid_v, par_sem.at[1])]
    for c in par:
        c.start()
    tabs = [
        pltpu.make_async_copy(src, dst, tab_sem.at[k])
        for k, (src, dst) in enumerate((
            (whole, whole_v), (points, points_v), (moment, moment_v), (inner, inner_v), (spread, spread_v)
        ))
    ]

    arrays = ((gate, g_v), (ograd, o_v), (xin, x_v))

    def fetch(q, which):
        return [
            pltpu.make_async_copy(arrays[k][0].at[:, q], arrays[k][1].at[q], in_sem.at[k, q]) for k in which
        ]

    for c in fetch(0, (0, 1)):
        c.start()
    tabs[0].start()
    for q in range(1, steps):
        for c in fetch(q, (0, 1)):
            c.start()
    for c in tabs[1:4]:
        c.start()
    for q in range(steps):
        fetch(q, (2,))[0].start()
    tabs[4].start()

    own[...] = jnp.zeros_like(own)
    stack[...] = jnp.zeros_like(stack)
    for c in par:
        c.wait()
    own[0, :, 0:16] = rate_v[...]
    own[1, :, 0:16] = resid_v[...]
    for i in range(2):
        row = own[i, 0:1]
        for c in range(1, 8):
            row = row + pltpu.roll(own[i, c : c + 1], 128 - 16 * c, 1)
        pack[i : i + 1] = row
    row = own[0, 0:1]
    for c in range(1, 8):
        row = row + pltpu.roll(own[0, c : c + 1], 16 * c, 1)
    rates[me] = pack[...]

    lane = lax.broadcasted_iota(jnp.int32, (8, 128), 1)
    group, place = lane // 16, lax.broadcasted_iota(jnp.int32, (8, 128), 0)

    def to_rows(block, count, dst):
        turned = block.T
        for e in range(n):
            tile = pltpu.roll(turned[8 * e : 8 * e + 8], 0, 1, stride=16, stride_axis=0)
            for i in range(count):
                line = jnp.sum(jnp.where(group == (place + i) % 8, tile, 0.0), axis=0, keepdims=True)
                dst[e, i : i + 1] = line if i == 0 else pltpu.roll(line, 128 - 16 * i, 1)

    tabs[0].wait()
    for q in range(steps):
        for c in fetch(q, (0, 1)):
            c.wait()
        s = (o_v[q].astype(f32) * g_v[q].astype(f32)).astype(bf16).reshape(256, 256)
        s_v[q] = s
        part = jnp.dot(whole_v[q], s, preferred_element_type=f32)
        sums = part if q == 0 else sums + part
    stack[0:POINTS] = sums[0:POINTS] + sums[POINTS:]
    to_rows(stack[...], POINTS // 16, mbuf)
    mgot[me] = mbuf[me]

    tabs[1].wait()
    falls = jnp.exp(points_v[...] * (-row))
    square = (128, 128)
    same = lax.broadcasted_iota(jnp.int32, square, 0) // 16 == lax.broadcasted_iota(jnp.int32, square, 1) // 16
    for i in range(POINTS // 16):
        part = jnp.concatenate([falls[16 * i : 16 * i + 16]] * 8, axis=0)
        table[128 * i : 128 * i + 128] = jnp.where(same, part, 0.0)

    pl.semaphore_wait(barrier, n - 1)
    others(lambda e: put(mbuf.at[e], mgot.at[me], m_send, m_recv, e))
    others(lambda e: put(pack, rates.at[me], rates_send, rates_recv, e))

    for k in range(TERMS):
        gacc[k] = jnp.zeros_like(gacc[k])
    tabs[2].wait()
    tabs[3].wait()

    def first(q, carry):
        fetch(q, (2,))[0].wait()
        s = s_v[q]
        x = x_v[q].reshape(256, 256)
        m_s[q] = jnp.dot(moment_v[...], s, preferred_element_type=f32)
        n_s[q] = jnp.dot(moment_v[...], x, preferred_element_type=f32)
        wide = x.astype(f32)
        for k in range(TERMS):
            near = jnp.dot(inner_v[k], s, preferred_element_type=f32)
            gacc[k] += jnp.sum((near * wide).reshape(32, 8, 256), axis=0)
        return carry

    lax.fori_loop(0, steps, first, 0)

    arrived(mgot.at[pl.ds(0, n - 1)], m_recv)
    sums = jnp.concatenate([mgot[:, i, :] for i in range(POINTS // 16)], axis=1)
    v = jnp.dot(sums, table[...], precision=lax.Precision.HIGHEST, preferred_element_type=f32)
    big = jnp.exp(row * (-float(span)))
    for by in (1, 2, 4, 8, 16):
        v = v + big * shift_rows(v, by)
        big = big * big
    states = shift_rows(v, 1)
    wide_group = lax.broadcasted_iota(jnp.int32, (n, 128), 1) // 16
    mirrored = states
    for c in range(1, 8):
        mirrored = jnp.where(wide_group == 8 - c, pltpu.roll(states, (128 - 32 * c) % 128, 1), mirrored)
    ubuf[:, 0, :] = mirrored
    ugot[me] = ubuf[me]
    others(lambda e: put(ubuf.at[e], ugot.at[me], u_send, u_recv, e))

    arrived(rates.at[pl.ds(0, n - 1)], rates_recv)
    def to_modes(row_of):
        tiles = [
            pltpu.roll(jnp.broadcast_to(row_of(e), (8, 128)), 0, 1, stride=16, stride_axis=0) for e in range(n)
        ]
        return jnp.concatenate(tiles, axis=0).T[0:16]

    lam = to_modes(lambda e: rates[e, 0:1])
    lam_s[...] = lam
    lamh_s[0:16] = lam[:, 0:128]
    lamh_s[16:32] = lam[:, 128:256]
    a32_s[...] = jnp.exp(-WIDTH * lam)
    a256_s[...] = jnp.exp(-chunk * lam)
    ahead = jnp.exp(-CENTER * lam)
    behind = jnp.exp(-(WIDTH - CENTER) * lam)
    h = lam * (WIDTH / 4)
    w = h * h
    power = jnp.ones_like(h)
    for k in range(TERMS):
        tail = 1.0 + w * (1.0 / (4 * (k + 4)))
        for m in (3, 2, 1):
            tail = 1.0 + w * tail * (1.0 / (m * (k + m)))
        term = power * tail * ((1.0 if k == 0 else 2.0) / math.factorial(k))
        e = ahead * (term if k % 2 == 0 else -term)
        b = behind * term
        en[k] = e
        fx[k] = b
        power = power * h

    def scan(r, carry):
        row = pl.ds(r, 1)
        e = [en[k, row, :] for k in range(TERMS)]
        a = a32_s[row, :]
        u = None
        for q in reversed(range(steps)):
            new = e[0] * m_s[q, 0:8]
            for k in range(1, TERMS):
                new = new + e[k] * m_s[q, 8 * k : 8 * k + 8]
            sq[q, r] = new
            u = new if u is None else new + a * u
        big = a256_s[row, :]
        for by in (1, 2, 4):
            u = u + big * shift_rows(u, by)
            big = big * big
        cin[r] = shift_rows(u, 1)
        return carry

    lax.fori_loop(0, 16, scan, 0, unroll=2)

    behind_chunks = (7 - lax.broadcasted_iota(jnp.int32, (8, 256), 0)).astype(f32) * (-float(chunk))
    gsum = [jnp.sum(gacc[k], axis=0, keepdims=True) for k in range(TERMS)]

    def share(r, carry):
        row = pl.ds(r, 1)
        f = [fx[k, row, :] for k in range(TERMS)]
        a = a32_s[row, :]
        reach = jnp.exp(behind_chunks * lam_s[row, :])
        p256[r] = reach
        u = cin[r]
        acc = jnp.zeros((8, 256), f32)
        tail = jnp.zeros((8, 256), f32)
        fall = jnp.ones((1, 256), f32)
        for q in reversed(range(steps)):
            v = f[0] * n_s[q, 0:8]
            for k in range(1, TERMS):
                v = v + f[k] * n_s[q, 8 * k : 8 * k + 8]
            acc = acc + v * u
            tail = tail + v * fall
            if q:
                u = sq[q, r] + a * u
                fall = fall * a
        near = jnp.sum(acc, axis=0, keepdims=True)
        for k in range(TERMS):
            near = near + en[k, row, :] * gsum[k]
        stack[row] = near
        stack[pl.ds(16 + r, 1)] = jnp.sum(tail * reach, axis=0, keepdims=True)
        return carry

    lax.fori_loop(0, 16, share, 0, unroll=2)

    to_rows(stack[...], 2, rbuf)
    rgot[me] = rbuf[me]
    others(lambda e: put(rbuf.at[e], rgot.at[me], r_send, r_recv, e))

    res = to_modes(lambda e: rates[e, 1:2])
    for k in range(TERMS):
        fo[k] = fx[k] * res
        tau[k] = jnp.sum(en[k] * res, axis=0, keepdims=True)

    def within(q, carry):
        s = s_v[q]
        acc = tau[0] * jnp.dot(inner_v[0], s, preferred_element_type=f32)
        for k in range(1, TERMS):
            acc = acc + tau[k] * jnp.dot(inner_v[k], s, preferred_element_type=f32)
        yin[q] = acc
        return carry

    lax.fori_loop(0, steps, within, 0, unroll=2)
    tabs[4].wait()

    arrived(ugot.at[pl.ds(0, n - 1)], u_recv)
    turned = to_modes(lambda e: ugot[e])
    for r in range(16):
        st[r] = cin[r] + p256[r] * turned[r : r + 1]

    for q in reversed(range(steps)):
        levels = [jnp.zeros((8, 256), f32)] * TERMS
        for r in range(16):
            u = st[r]
            for k in range(TERMS):
                levels[k] = levels[k] + fo[k, r : r + 1, :] * u
            if q:
                st[r] = sq[q, r] + a32_s[r : r + 1, :] * u
        level = jnp.concatenate(levels, axis=0)
        high = level.astype(bf16)
        low = (level - high.astype(f32)).astype(bf16)
        both = jnp.concatenate([high, low], axis=0)
        y = yin[q] + jnp.dot(spread_v[...], both, preferred_element_type=f32)
        out[:, q] = y.astype(bf16).reshape(CHUNKS, WIDTH, 256)

    arrived(rgot.at[pl.ds(0, n - 1)], r_recv)
    total = jnp.sum(rgot[:, 0, :] + rgot[:, 1, :] * states, axis=0, keepdims=True)
    total = total * (1.0 / length)
    for c in range(8):
        moved = total if c == 0 else pltpu.roll(total, 128 - 16 * c, 1)
        rgrad[c : c + 1] = moved[:, 0:16]

    arrived(rates.at[pl.ds(0, n - 1)], rates_send)
    arrived(mgot.at[pl.ds(0, n - 1)], m_send)
    arrived(ugot.at[pl.ds(0, n - 1)], u_send)
    arrived(rgot.at[pl.ds(0, n - 1)], r_send)


def store(y, r, out, rgrad, sems):
    parts = y.shape[0]
    copies = [pltpu.make_async_copy(r, rgrad, sems.at[parts])]
    copies += [pltpu.make_async_copy(y.at[j], out.at[j], sems.at[j]) for j in range(parts)]
    for c in copies:
        c.start()
    for c in copies:
        c.wait()


def local(inner, moment, spread, whole, points, gate_value, conv_input, output_grad, decay_rate, residue):
    tokens, channels = gate_value.shape
    n = lax.axis_size("ctx")
    steps = tokens // (CHUNKS * WIDTH)
    cut = (CHUNKS, steps, WIDTH, channels)
    V = pltpu.VMEM
    dma = pltpu.SemaphoreType.DMA
    blocks = (steps, CHUNKS, WIDTH, channels)
    size = CHUNKS * WIDTH
    scratch = [
        V(blocks, bf16), V(blocks, bf16), V(blocks, bf16), V((steps, size, channels), bf16),
        V(inner.shape, bf16), V(moment.shape, bf16), V(spread.shape, bf16), V(whole.shape, bf16), V(points.shape, f32), V((8, 16), f32), V((8, 16), f32),
        V((2, 8, 128), f32), V((2, 128), f32), V((n, 2, 128), f32),
        V((steps, TERMS * CHUNKS, channels), f32), V((steps, TERMS * CHUNKS, channels), f32),
        V((TERMS, 8, channels), f32), V((TERMS, 1, channels), f32),
        V((TERMS, 16, channels), f32), V((TERMS, 16, channels), f32), V((TERMS, 16, channels), f32),
        V((16, channels), f32), V((16, channels), f32), V((16, channels), f32), V((32, 128), f32),
        V((steps, 16, 8, channels), f32), V((16, 8, channels), f32), V((16, 8, channels), f32), V((16, 8, channels), f32),
        V((steps, size, channels), f32), V((128, channels), f32),
        V((8 * POINTS, 128), f32), V((n, POINTS // 16, 128), f32), V((n, POINTS // 16, 128), f32),
        V((n, 1, 128), f32), V((n, 1, 128), f32), V((n, 2, 128), f32), V((n, 2, 128), f32),
        dma((3, steps)), dma((5,)), dma((2,)),
    ] + [dma] * 8
    vmem_spec = pl.BlockSpec(memory_space=pltpu.VMEM)
    hbm_spec = pl.BlockSpec(memory_space=pltpu.HBM)
    out, rgrad = pl.pallas_call(
        functools.partial(kernel, n, tokens * n),
        out_shape=(jax.ShapeDtypeStruct(cut, bf16), jax.ShapeDtypeStruct(residue.shape, f32)),
        in_specs=[hbm_spec] * 10,
        out_specs=(vmem_spec, vmem_spec),
        scratch_shapes=scratch,
        compiler_params=pltpu.CompilerParams(
            collective_id=0, has_side_effects=True, vmem_limit_bytes=24 * 1024 * 1024
        ),
    )(*[
        pltpu.with_memory_space_constraint(a, pltpu.HBM)
        for a in (
            gate_value.reshape(cut), conv_input.reshape(cut), output_grad.reshape(cut),
            decay_rate, residue, inner, moment, spread, whole, points,
        )
    ])
    out, rgrad = pl.pallas_call(
        store,
        out_shape=(jax.ShapeDtypeStruct(cut, bf16), jax.ShapeDtypeStruct(residue.shape, f32)),
        in_specs=[vmem_spec] * 2,
        out_specs=(hbm_spec, hbm_spec),
        scratch_shapes=[dma((CHUNKS + 1,))],
    )(*[pltpu.with_memory_space_constraint(a, pltpu.VMEM) for a in (out, rgrad)])
    return out.reshape(tokens, channels), rgrad


def solution(mesh):
    consts = tables(8)
    in_specs = (P(),) * 5 + (P("ctx", "fsdp"),) * 3 + (P(("fsdp", "ctx"), None),) * 2
    out_specs = (P("ctx", "fsdp"), P(("fsdp", "ctx"), None))
    mapped = jax.shard_map(local, mesh=mesh, in_specs=in_specs, out_specs=out_specs, check_vma=False)

    def run(*args):
        return mapped(*[jnp.asarray(c) for c in consts], *args)

    return run
```
